32 devices in a mesh: vox: 8 (over y, x, core), tm: 4 (over z).
Axes of the slice: x: 2, y: 2, z: 4, core: 2. Of those that a mesh axis runs over, the one named last changes fastest.
Arguments:
- series: float32 [2048, 16384], P('tm', 'vox'), may hold values from -40 to 40
- spikes: int32 [2048, 16384], P('tm', 'vox'), may hold values from 0 to 15
- motion: float32 [2048, 6], P('tm'), may hold values from -5 to 5
- tissue: float32 [3, 16384], P(None, 'vox'), may hold values from 0.01 to 12, as said below
Outputs:
- cleaned: float32 [2048, 16384], P('tm', 'vox')
The draws below stay inside these ranges and needn't reach their ends.
Inputs may be any that keep to these rules, and one draw needn't show every extreme that they name: Bit j-1 of an entry (spikes // 2^(j-1) odd) flags that frame's level-j coefficient of that voxel as a spike. `tissue`: all weights are positive.
All inputs are finite; a program needn't handle non-finite values.
Results may differ from the reference program's by a relative error of at most 0.0003.
Values sent between devices are 32-bit elements; how exact they have to be, the bound alone decides.
A program may use at most 64 MiB of HBM per device.

```python
import jax
import jax.numpy as jnp
from jax import lax

FRAMES = 2048
LEVELS = 4
VOXELS = 16384
N_VOX = 8


def tissue_class(count):
    return jnp.arange(count, dtype=jnp.int32) // 64 % 3


def draw_series(key, part):
    keys = jax.random.split(jax.random.fold_in(key, 11), 5)
    regions = VOXELS // 64
    noise = jax.random.normal(keys[0], (FRAMES, VOXELS), jnp.float32)
    courses = jax.random.normal(keys[1], (FRAMES, regions), jnp.float32)
    loads = jax.random.uniform(keys[2], (VOXELS,), jnp.float32, 0.5, 1.5)
    common = jax.random.normal(keys[3], (FRAMES,), jnp.float32)
    class_courses = jax.random.normal(keys[4], (FRAMES, 3), jnp.float32)
    member = (tissue_class(VOXELS)[None, :] == jnp.arange(3, dtype=jnp.int32)[:, None]).astype(jnp.float32)
    own_course = jnp.dot(class_courses, member, precision=jax.lax.Precision.HIGHEST)
    regional = jnp.repeat(courses, 64, axis=1)
    mixed = noise + loads[None, :] * (0.8 * common[:, None] + 0.8 * regional + 0.8 * own_course)
    return jnp.clip(mixed, -40.0, 40.0)


def draw_tissue(key, part):
    keys = jax.random.split(jax.random.fold_in(key, 23), 1)
    base_regressors = jax.random.uniform(keys[0], (3, VOXELS), jnp.float32, 0.1, 1.0)
    place = jnp.arange(VOXELS, dtype=jnp.float32) / float(VOXELS - 1)
    member = tissue_class(VOXELS)[None, :] == jnp.arange(3, dtype=jnp.int32)[:, None]
    focus = jnp.where(member, 1.0, 0.15).astype(jnp.float32)
    ramp = 1.0 + 2.0 * place
    return base_regressors * ramp[None, :] * focus


def set_ends(result, rng, smallest, largest):
    shape = result.shape
    index_at = [jax.random.randint(jax.random.fold_in(rng, axis), (), 0, shape[axis]) for axis in range(len(shape))]
    result = result.at[tuple(index_at)].set(smallest)
    longest = shape.index(max(shape))
    index_at[longest] = (index_at[longest] + 1) % shape[longest]
    return result.at[tuple(index_at)].set(largest)


def block_scale(key, dims, shards, smallest, largest):
    gain = 1.0
    for axis_at, shards_of in shards:
        steps = jax.random.uniform(jax.random.fold_in(jax.random.fold_in(key, 6), axis_at), (shards_of,), jnp.float32, smallest / len(shards), largest / len(shards))
        gain = gain * jnp.repeat(jnp.exp(steps), dims[axis_at] // shards_of).reshape((-1,) + (1,) * (len(dims) - 1 - axis_at))
    return gain


def normal_values(rng, dims, scale, most, shards=(), held_as=jnp.bfloat16):
    result = jax.random.normal(rng, dims, jnp.float32) * scale
    if len(shards) > 0:
        result = block_scale(rng, dims, shards, -0.22, 0.18) * result
    return jnp.clip(result, min=-most, max=most).astype(held_as)


def setup_inputs(seed: int = 0) -> dict:
    streams_of = jax.random.split(jax.random.key(seed), 5)
    series = draw_series(jax.random.fold_in(streams_of[4], 71), 0)
    spikes = set_ends(jax.random.randint(streams_of[1], (FRAMES, VOXELS), 0, 16), jax.random.fold_in(streams_of[1], 1), 0, 15).astype(jnp.int32)
    motion = normal_values(streams_of[2], (FRAMES, 6), 1.0, 5.0, ((0, 4),), jnp.float32)
    tissue = draw_tissue(jax.random.fold_in(streams_of[4], 71), 0)
    return {"series": series, "spikes": spikes, "motion": motion, "tissue": tissue}


def precise_product(left, right):
    return jnp.dot(left.astype(jnp.float32), right.astype(jnp.float32), precision=lax.Precision.HIGHEST, preferred_element_type=jnp.float32)

def despike(voxel_block, flags):
    approx = voxel_block
    kept_list = []
    for level in range(LEVELS):
        shift_rows = 2 ** level
        keep = 1.0 - (flags // 2 ** level % 2).astype(jnp.float32)
        lagged = jnp.roll(approx, shift_rows, axis=0)
        detail = (approx - lagged) * 0.5
        kept_list.append(detail * keep)
        approx = (approx + lagged) * 0.5
    for level in range(LEVELS - 1, -1, -1):
        shift_rows = 2 ** level
        kept = kept_list[level]
        lead_approx = jnp.roll(approx, -shift_rows, axis=0)
        lead_kept = jnp.roll(kept, -shift_rows, axis=0)
        approx = (approx + lead_approx) * 0.5 + (kept - lead_kept) * 0.5
    return approx

def assemble_nuisance_matrix(motion, voxel_signals, previous_frames):
    base_regressors = jnp.concatenate([motion, voxel_signals], axis=1)
    before = jnp.concatenate([previous_frames, base_regressors[:-1]], axis=0)
    temporal_derivative = base_regressors - before
    return jnp.concatenate([base_regressors, temporal_derivative, base_regressors * base_regressors, temporal_derivative * temporal_derivative], axis=1)

def reference(series, spikes, motion, tissue):
    frames = series.shape[0]
    width = series.shape[1] // N_VOX

    def first_pass(index, carry):
        store, numer = carry
        start = jnp.asarray(index).astype(jnp.int32) * width
        voxel_block = lax.dynamic_slice_in_dim(series, start, width, 1)
        flags = lax.dynamic_slice_in_dim(spikes, start, width, 1)
        weights = lax.dynamic_slice_in_dim(tissue, start, width, 1)
        clean_block = despike(voxel_block, flags)
        numer = numer + precise_product(clean_block, weights.T)
        store = lax.dynamic_update_slice_in_dim(store, clean_block, start, 1)
        return (store, numer)
    store0 = jnp.zeros(series.shape, jnp.float32)
    numer0 = jnp.zeros((frames, 3), jnp.float32)
    spike_free_series, numer = lax.fori_loop(0, N_VOX, first_pass, (store0, numer0))
    voxel_signals = numer / float(VOXELS)
    nuisance_matrix = assemble_nuisance_matrix(motion, voxel_signals, jnp.zeros((1, 9), jnp.float32))
    gram_matrix = precise_product(nuisance_matrix.T, nuisance_matrix)
    factor = jnp.linalg.cholesky(gram_matrix)

    def second_pass(index, store):
        start = jnp.asarray(index).astype(jnp.int32) * width
        voxel_block = lax.dynamic_slice_in_dim(spike_free_series, start, width, 1)
        cross_products = precise_product(nuisance_matrix.T, voxel_block)
        beta_estimates = jax.scipy.linalg.cho_solve((factor, True), cross_products)
        residual_output = voxel_block - precise_product(nuisance_matrix, beta_estimates)
        return lax.dynamic_update_slice_in_dim(store, residual_output, start, 1)
    return lax.fori_loop(0, N_VOX, second_pass, jnp.zeros(series.shape, jnp.float32))
```

```python
import functools

import jax
import jax.numpy as jnp
from jax import lax
from jax.experimental import pallas as pl
from jax.experimental.pallas import tpu as pltpu
from jax.sharding import PartitionSpec as P

LEVELS = 4
HALO = 16
WIDE = 256
MESH = pl.DeviceIdType.MESH
HIGHEST = lax.Precision.HIGHEST


def split2(x):
    high = x.astype(jnp.bfloat16).astype(jnp.float32)
    return high, x - high


def nt(a, b, precision=None):
    return lax.dot_general(a, b, (((1,), (1,)), ((), ())), precision=precision, preferred_element_type=jnp.float32)


def nn(a, b, precision=None):
    return lax.dot_general(a, b, (((1,), (0,)), ((), ())), precision=precision, preferred_element_type=jnp.float32)


def despike_block(xs, sp, y, ym1, c, frames):
    q = frames // 8

    def rows(i):
        return pl.ds(HALO + i, 8, stride=q)

    approx = [dict() for _ in range(LEVELS + 1)]
    plus = [dict() for _ in range(LEVELS + 1)]
    kept = [dict() for _ in range(LEVELS + 1)]
    flags = {}
    reco = [dict() for _ in range(LEVELS + 1)]
    first = [-1 - 15 + 2**j - 1 for j in range(LEVELS + 1)]
    last = [q - 1 + 15] * (LEVELS + 1)
    for i in range(first[0], last[0] + 1):
        approx[0][i] = xs[c, rows(i), :]
        if i >= -1:
            flags[i] = sp[c, rows(i), :]
        for j in range(1, LEVELS + 1):
            if i < first[j]:
                continue
            s = 2 ** (j - 1)
            here, lag = approx[j - 1][i], approx[j - 1][i - s]
            approx[j][i] = here + lag
            if -1 <= i <= q - 1 + (2**j - 1):
                detail = (here - lag) * (4.0 ** (LEVELS - j)) if j < LEVELS else here - lag
                kept[j][i] = jnp.where((flags[i] & s) == 0, detail, 0.0)
        t = i
        if t < -1:
            continue
        reco[LEVELS][t] = approx[LEVELS][t]
        for j in range(LEVELS, 0, -1):
            s = 2 ** (j - 1)
            if t > q - 1 + (2**j - 1):
                break
            plus[j][t] = reco[j][t] + kept[j][t]
            minus = reco[j][t] - kept[j][t]
            t = t - s
            if t < -1:
                break
            reco[j - 1][t] = plus[j][t] + minus
            if j == 1:
                value = reco[0][t] * (0.5 ** (2 * LEVELS))
                if t >= 0:
                    y[c, pl.ds(t, 8, stride=q), :] = value
                else:
                    ym1[:, pl.ds(pl.multiple_of(c * 128, 128), 128)] = value


def kernel(n_vox, n_tm, series, spikes, mt_ref, tissue_ref, y_out, cs_out, bs_out,
           xs, sp, y, ym1, yh, yl, mprev, own_m, in_rm, in_lm, out_rm, out_lm,
           own_s, in_rs, in_ls, out_rs, out_ls, sig, sig_in, gram, gram_in, wbuf, cmb, sacc,
           loc_sem, halo_send, halo_recv, mp_sem, rm_send, rm_recv, lm_send, lm_recv,
           rs_send, rs_recv, ls_send, ls_recv, sig_send, sig_recv, gr_send, gr_recv, y_sem):
    frames, cols = series.shape
    groups = cols // WIDE
    blocks = cols // 128
    p = lax.axis_index("tm")
    v = lax.axis_index("vox")
    right = lax.rem(p + 1, n_tm)
    left = lax.rem(p + n_tm - 1, n_tm)

    def at(g):
        return pl.ds(pl.multiple_of(g * WIDE, WIDE), WIDE)

    def lanes(c):
        return pl.ds(pl.multiple_of(c * 128, 128), 128)

    def local_copies(c):
        return (
            pltpu.make_async_copy(series.at[:, lanes(c)], xs.at[c, pl.ds(HALO, frames)], loc_sem.at[0, c]),
            pltpu.make_async_copy(spikes.at[:, lanes(c)], sp.at[c, pl.ds(HALO, frames)], loc_sem.at[1, c]),
        )

    def halo_copies(c):
        def copy(k, src, dst, target):
            return pltpu.make_async_remote_copy(
                src_ref=src, dst_ref=dst, send_sem=halo_send.at[k, c], recv_sem=halo_recv.at[k, c],
                device_id=(v, target), device_id_type=MESH)
        return (
            copy(0, series.at[pl.ds(frames - HALO, HALO), lanes(c)], xs.at[c, pl.ds(0, HALO)], right),
            copy(1, spikes.at[pl.ds(frames - 8, 8), lanes(c)], sp.at[c, pl.ds(HALO - 8, 8)], right),
            copy(2, series.at[pl.ds(0, HALO), lanes(c)], xs.at[c, pl.ds(HALO + frames, HALO)], left),
            copy(3, spikes.at[pl.ds(0, HALO), lanes(c)], sp.at[c, pl.ds(HALO + frames, HALO)], left),
        )

    @pl.loop(0, blocks)
    def _(c):
        for copy in local_copies(c):
            copy.start()

    barrier = pltpu.get_barrier_semaphore()
    for k in range(1, n_vox):
        pl.semaphore_signal(barrier, inc=1, device_id=(lax.rem(v + k, n_vox), p), device_id_type=MESH)
    for k in range(1, n_tm):
        pl.semaphore_signal(barrier, inc=1, device_id=(v, lax.rem(p + k, n_tm)), device_id_type=MESH)
    pl.semaphore_wait(barrier, n_vox - 1 + n_tm - 1)

    mp = pltpu.make_async_remote_copy(
        src_ref=mt_ref.at[:, pl.ds(frames - 128, 128)], dst_ref=mprev, send_sem=mp_sem.at[0], recv_sem=mp_sem.at[1],
        device_id=(v, right), device_id_type=MESH)
    mp.start()

    @pl.loop(0, blocks)
    def _(c):
        for copy in halo_copies(c):
            copy.start()

    @pl.when(p == 0)
    def _():
        in_rm[...] = jnp.zeros_like(in_rm)
        in_rs[...] = jnp.zeros_like(in_rs)

    @pl.when(p == n_tm - 1)
    def _():
        in_lm[...] = jnp.zeros_like(in_lm)
        in_ls[...] = jnp.zeros_like(in_ls)

    w = tissue_ref[...]
    w_high, w_low = split2(w)
    pad = jnp.zeros((5, cols), jnp.float32)
    wbuf[...] = jnp.concatenate([w_high, pad, w_low, pad], axis=0).astype(jnp.bfloat16)
    lane_at = lax.broadcasted_iota(jnp.int32, (8, frames), 1)
    later = jnp.where(p > 0, 1.0, 0.0).astype(jnp.float32)

    def derivative(base, before):
        return base - jnp.where(lane_at == 0, before * later, pltpu.roll(base, 1, 1))

    mp.wait()
    base = mt_ref[...]
    deriv = derivative(base, mprev[:, 127:128])
    conf_m = jnp.concatenate([base[:6], deriv[:6], (base * base)[:6], (deriv * deriv)[:6]], axis=0)
    cmb[...] = jnp.concatenate(split2(conf_m), axis=0).astype(jnp.bfloat16)
    sacc[...] = jnp.zeros_like(sacc)

    def scan_copy(src, dst, send, recv, r, target):
        return pltpu.make_async_remote_copy(
            src_ref=src.at[r], dst_ref=dst.at[r], send_sem=send.at[r], recv_sem=recv.at[r],
            device_id=(v, target), device_id_type=MESH)

    def forward(step, count, own, ins, outs, sends, recvs):
        for way, (first_at, end_at, target) in enumerate(((p, n_tm - 1, right), (n_tm - 1 - p, 0, left))):
            r = step - first_at

            @pl.when((r >= 0) & (r < count))
            def _():
                copy = scan_copy(outs[way], ins[way], sends[way], recvs[way], r, target)

                @pl.when(first_at > 0)
                def _():
                    copy.wait_recv()

                @pl.when(p != end_at)
                def _():
                    outs[way][r] = own[r] + ins[way][r]
                    copy.start()

    m_args = (own_m, (in_rm, in_lm), (out_rm, out_lm), (rm_send, lm_send), (rm_recv, lm_recv))
    s_args = (own_s, (in_rs, in_ls), (out_rs, out_ls), (rs_send, ls_send), (rs_recv, ls_recv))

    def y_copy(c):
        return pltpu.make_async_copy(y.at[c], y_out.at[:, lanes(c)], y_sem.at[c])

    @pl.loop(0, groups)
    def _(g):
        @pl.loop(0, 2)
        def _(k):
            c = 2 * g + k
            for copy in local_copies(c):
                copy.wait()
            for copy in halo_copies(c):
                copy.wait_recv()
            despike_block(xs, sp, y, ym1, c, frames)
            y_copy(c).start()

        block = jnp.concatenate([y[2 * g], y[2 * g + 1]], axis=1)
        high = block.astype(jnp.bfloat16)
        low = (block - high.astype(jnp.float32)).astype(jnp.bfloat16)
        yh[:, at(g)] = high
        yl[:, at(g)] = low
        wg = wbuf[:, at(g)]
        sacc[...] += nt(wg, high) + nt(wg, low)
        cross = nn(cmb[...], high) + nn(cmb[...], low)
        own_m[g] = cross[:24] + cross[24:]
        forward(g, groups, *m_args)

    sig[:, pl.ds(0, frames)] = sacc[0:8] + sacc[8:16]
    edge = jnp.sum(ym1[0:1] * tissue_ref[...], axis=1, keepdims=True)
    sig[0:3, pl.ds(frames, 128)] = jnp.broadcast_to(edge, (3, 128))
    sig[3:8, pl.ds(frames, 128)] = jnp.zeros((5, 128), jnp.float32)

    def sig_copy(k):
        return pltpu.make_async_remote_copy(
            src_ref=sig, dst_ref=sig_in.at[k], send_sem=sig_send.at[k], recv_sem=sig_recv.at[k],
            device_id=(lax.rem(v + k + 1, n_vox), p), device_id_type=MESH)

    for k in range(n_vox - 1):
        sig_copy(k).start()

    @pl.loop(groups, groups + n_tm - 1)
    def _(step):
        forward(step, groups, *m_args)

    total = sig[...]
    for k in range(n_vox - 1):
        sig_copy(k).wait()
        total = total + sig_in[k]
    total = total * (1.0 / float(cols * n_vox))
    base = total[:, :frames]
    deriv = derivative(base, total[:, frames:frames + 1])
    conf_s = jnp.concatenate(
        [base[:3], deriv[:3], (base * base)[:3], (deriv * deriv)[:3], jnp.zeros((4, frames), jnp.float32)], axis=0)
    csb = jnp.concatenate(split2(conf_s), axis=0).astype(jnp.bfloat16)
    base = mt_ref[...]
    deriv = derivative(base, mprev[:, 127:128])
    conf_m = jnp.concatenate([base[:6], deriv[:6], (base * base)[:6], (deriv * deriv)[:6]], axis=0)
    conf = jnp.concatenate([conf_m, conf_s], axis=0)
    gram[...] = nt(conf, jnp.concatenate([conf, jnp.zeros((88, frames), jnp.float32)], axis=0), HIGHEST)

    def gram_copy(k):
        return pltpu.make_async_remote_copy(
            src_ref=gram, dst_ref=gram_in.at[k], send_sem=gr_send.at[k], recv_sem=gr_recv.at[k],
            device_id=(v, lax.rem(p + k + 1, n_tm)), device_id_type=MESH)

    for k in range(n_tm - 1):
        gram_copy(k).start()

    for g in range(groups):
        part = pl.ds(g * WIDE, WIDE)
        cross = nn(csb, yh[:, part]) + nn(csb, yl[:, part])
        own_s[g] = cross[:16] + cross[16:]
        forward(g, groups, *s_args)

    conf48 = jnp.concatenate([conf, jnp.zeros((8, frames), jnp.float32)], axis=0)
    c_high, c_low = split2(conf48)
    cs_out[...] = jnp.concatenate([c_high, c_low, c_high], axis=0).astype(jnp.bfloat16)

    matrix = gram[...]
    for k in range(n_tm - 1):
        gram_copy(k).wait()
        matrix = matrix + gram_in[k]
    row_at = lax.broadcasted_iota(jnp.int32, (40, 128), 0)
    col_at = lax.broadcasted_iota(jnp.int32, (40, 128), 1)
    for k in range(36):
        pivot_row = matrix[k:k + 1, :]
        pivot_col = matrix[:, k:k + 1]
        inverse = 1.0 / pivot_row[:, k:k + 1]
        scaled = jnp.where(col_at[0:1] == k, inverse, pivot_row * inverse)
        rest = jnp.where(col_at == k, 0.0, matrix)
        matrix = jnp.where(row_at == k, scaled, rest - pivot_col * scaled)

    @pl.loop(groups, groups + n_tm - 1)
    def _(step):
        forward(step, groups, *s_args)

    inv = matrix[:, :40]
    for g in range(groups):
        cross = jnp.concatenate(
            [own_m[g] + in_rm[g] + in_lm[g], own_s[g] + in_rs[g] + in_ls[g]], axis=0)
        coef = nn(inv, cross, HIGHEST)
        b_high, b_low = split2(jnp.concatenate([coef, jnp.zeros((8, WIDE), jnp.float32)], axis=0))
        bs_out[:, pl.ds(g * WIDE, WIDE)] = jnp.concatenate([b_high, b_high, b_low], axis=0).astype(jnp.bfloat16)

    @pl.loop(0, groups)
    def _(g):
        for k in range(2):
            y_copy(2 * g + k).wait()
            for copy in halo_copies(2 * g + k):
                copy.wait_send()
        for args in (m_args, s_args):
            for way, (end_at, target) in enumerate(((n_tm - 1, right), (0, left))):
                @pl.when(p != end_at)
                def _():
                    scan_copy(args[2][way], args[1][way], args[3][way], args[4][way], g, target).wait_send()


def apply_kernel(y_ref, cs_ref, bs_ref, out_ref):
    out_ref[...] = y_ref[...] - lax.dot_general(
        cs_ref[...], bs_ref[...], (((0,), (0,)), ((), ())), preferred_element_type=jnp.float32)


def local(n_vox, n_tm, series, spikes, motion, tissue):
    frames, cols = series.shape
    groups = cols // WIDE
    blocks = cols // 128
    mt = jnp.pad(motion.T, ((0, 2), (0, 0)))
    f32, bf16 = jnp.float32, jnp.bfloat16
    vmem = pl.BlockSpec(memory_space=pltpu.VMEM)
    hbm = pl.BlockSpec(memory_space=pl.ANY)
    dma = pltpu.SemaphoreType.DMA
    sums_m = pltpu.VMEM((groups, 24, WIDE), f32)
    sums_s = pltpu.VMEM((groups, 16, WIDE), f32)
    y, cs, bs = pl.pallas_call(
        functools.partial(kernel, n_vox, n_tm),
        out_shape=(
            jax.ShapeDtypeStruct((frames, cols), f32),
            jax.ShapeDtypeStruct((144, frames), bf16),
            jax.ShapeDtypeStruct((144, cols), bf16),
        ),
        in_specs=[hbm, hbm, vmem, vmem],
        out_specs=[hbm, vmem, vmem],
        scratch_shapes=[
            pltpu.VMEM((blocks, frames + 2 * HALO, 128), f32),
            pltpu.VMEM((blocks, frames + 2 * HALO, 128), jnp.int32),
            pltpu.VMEM((blocks, frames, 128), f32),
            pltpu.VMEM((8, cols), f32),
            pltpu.VMEM((frames, cols), bf16),
            pltpu.VMEM((frames, cols), bf16),
            pltpu.VMEM((8, 128), f32),
            sums_m, sums_m, sums_m, sums_m, sums_m,
            sums_s, sums_s, sums_s, sums_s, sums_s,
            pltpu.VMEM((8, frames + 128), f32),
            pltpu.VMEM((n_vox - 1, 8, frames + 128), f32),
            pltpu.VMEM((40, 128), f32),
            pltpu.VMEM((n_tm - 1, 40, 128), f32),
            pltpu.VMEM((16, cols), bf16),
            pltpu.VMEM((48, frames), bf16),
            pltpu.VMEM((16, frames), f32),
            dma((2, blocks)), dma((4, blocks)), dma((4, blocks)), dma((2,)),
            dma((groups,)), dma((groups,)), dma((groups,)), dma((groups,)),
            dma((groups,)), dma((groups,)), dma((groups,)), dma((groups,)),
            dma((n_vox - 1,)), dma((n_vox - 1,)), dma((n_tm - 1,)), dma((n_tm - 1,)),
            dma((blocks,)),
        ],
        compiler_params=pltpu.CompilerParams(
            collective_id=0, has_side_effects=True, vmem_limit_bytes=48 * 1024 * 1024),
        cost_estimate=pl.CostEstimate(flops=10**9, bytes_accessed=12 * frames * cols, transcendentals=0),
        name="despike_and_fit",
    )(series, spikes, mt, tissue)
    return pl.pallas_call(
        apply_kernel,
        grid=(groups,),
        out_shape=jax.ShapeDtypeStruct((frames, cols), f32),
        in_specs=[
            pl.BlockSpec((frames, WIDE), lambda g: (0, g)),
            pl.BlockSpec((144, frames), lambda g: (0, 0)),
            pl.BlockSpec((144, WIDE), lambda g: (0, g)),
        ],
        out_specs=pl.BlockSpec((frames, WIDE), lambda g: (0, g)),
        compiler_params=pltpu.CompilerParams(vmem_limit_bytes=32 * 1024 * 1024),
        name="apply_coefficients",
    )(y, cs, bs)


def solution(mesh):
    return jax.shard_map(
        functools.partial(local, mesh.shape["vox"], mesh.shape["tm"]),
        mesh=mesh,
        in_specs=(P("tm", "vox"), P("tm", "vox"), P("tm", None), P(None, "vox")),
        out_specs=P("tm", "vox"),
        check_vma=False,
    )
```

```python
import functools

import jax
import jax.numpy as jnp
from jax import lax
from jax.experimental import pallas as pl
from jax.experimental.pallas import tpu as pltpu
from jax.sharding import PartitionSpec as P

LEVELS = 4
HALO = 16
WIDE = 256
LAG_M = 4
LAG_S = 4
APPLY = 512
MESH = pl.DeviceIdType.MESH
HIGHEST = lax.Precision.HIGHEST


def split2(x):
    high = x.astype(jnp.bfloat16).astype(jnp.float32)
    return high, x - high


def nt(a, b, precision=None):
    return lax.dot_general(a, b, (((1,), (1,)), ((), ())), precision=precision, preferred_element_type=jnp.float32)


def nn(a, b, precision=None):
    return lax.dot_general(a, b, (((1,), (0,)), ((), ())), precision=precision, preferred_element_type=jnp.float32)


def despike_block(xs, sp, y, ym1, c, frames):
    q = frames // 8

    def rows(i):
        return pl.ds(HALO + i, 8, stride=q)

    approx = [dict() for _ in range(LEVELS + 1)]
    plus = [dict() for _ in range(LEVELS + 1)]
    kept = [dict() for _ in range(LEVELS + 1)]
    flags = {}
    reco = [dict() for _ in range(LEVELS + 1)]
    first = [-1 - 15 + 2**j - 1 for j in range(LEVELS + 1)]
    last = [q - 1 + 15] * (LEVELS + 1)
    for i in range(first[0], last[0] + 1):
        approx[0][i] = xs[c, rows(i), :]
        if i >= -1:
            flags[i] = sp[c, rows(i), :]
        for j in range(1, LEVELS + 1):
            if i < first[j]:
                continue
            s = 2 ** (j - 1)
            here, lag = approx[j - 1][i], approx[j - 1][i - s]
            approx[j][i] = here + lag
            if -1 <= i <= q - 1 + (2**j - 1):
                detail = (here - lag) * (4.0 ** (LEVELS - j)) if j < LEVELS else here - lag
                kept[j][i] = jnp.where((flags[i] & s) == 0, detail, 0.0)
        t = i
        if t < -1:
            continue
        reco[LEVELS][t] = approx[LEVELS][t]
        for j in range(LEVELS, 0, -1):
            s = 2 ** (j - 1)
            if t > q - 1 + (2**j - 1):
                break
            plus[j][t] = reco[j][t] + kept[j][t]
            minus = reco[j][t] - kept[j][t]
            t = t - s
            if t < -1:
                break
            reco[j - 1][t] = plus[j][t] + minus
            if j == 1:
                value = reco[0][t] * (0.5 ** (2 * LEVELS))
                if t >= 0:
                    y[c, pl.ds(t, 8, stride=q), :] = value
                else:
                    ym1[:, pl.ds(pl.multiple_of(c * 128, 128), 128)] = value


def kernel(n_vox, n_tm, series, spikes, mt_ref, tissue_ref, y_out, cs_out, bs_out,
           xs, sp, y, ym1, yh, yl, mprev, own_m, in_rm, in_lm, out_rm, out_lm,
           own_s, in_rs, in_ls, out_rs, out_ls, sig, sig_in, gram, gram_in, wbuf, cmb, sacc,
           loc_sem, halo_send, halo_recv, mp_sem, rm_send, rm_recv, lm_send, lm_recv,
           rs_send, rs_recv, ls_send, ls_recv, sig_send, sig_recv, gr_send, gr_recv, y_sem):
    frames, cols = series.shape
    groups = cols // WIDE
    blocks = cols // 128
    p = lax.axis_index("tm")
    v = lax.axis_index("vox")
    right = lax.rem(p + 1, n_tm)
    left = lax.rem(p + n_tm - 1, n_tm)

    def at(g):
        return pl.ds(pl.multiple_of(g * WIDE, WIDE), WIDE)

    def lanes(c):
        return pl.ds(pl.multiple_of(c * 128, 128), 128)

    def local_copies(c):
        return (
            pltpu.make_async_copy(series.at[:, lanes(c)], xs.at[c, pl.ds(HALO, frames)], loc_sem.at[0, c]),
            pltpu.make_async_copy(spikes.at[:, lanes(c)], sp.at[c, pl.ds(HALO, frames)], loc_sem.at[1, c]),
        )

    def halo_copies(c):
        def copy(k, src, dst, target):
            return pltpu.make_async_remote_copy(
                src_ref=src, dst_ref=dst, send_sem=halo_send.at[k, c], recv_sem=halo_recv.at[k, c],
                device_id=(v, target), device_id_type=MESH)
        return (
            copy(0, series.at[pl.ds(frames - HALO, HALO), lanes(c)], xs.at[c, pl.ds(0, HALO)], right),
            copy(1, spikes.at[pl.ds(frames - 8, 8), lanes(c)], sp.at[c, pl.ds(HALO - 8, 8)], right),
            copy(2, series.at[pl.ds(0, HALO), lanes(c)], xs.at[c, pl.ds(HALO + frames, HALO)], left),
            copy(3, spikes.at[pl.ds(0, HALO), lanes(c)], sp.at[c, pl.ds(HALO + frames, HALO)], left),
        )

    @pl.loop(0, blocks)
    def _(c):
        for copy in local_copies(c):
            copy.start()

    barrier = pltpu.get_barrier_semaphore()
    for k in range(1, n_vox):
        pl.semaphore_signal(barrier, inc=1, device_id=(lax.rem(v + k, n_vox), p), device_id_type=MESH)
    for k in range(1, n_tm):
        pl.semaphore_signal(barrier, inc=1, device_id=(v, lax.rem(p + k, n_tm)), device_id_type=MESH)
    pl.semaphore_wait(barrier, n_vox - 1 + n_tm - 1)

    mp = pltpu.make_async_remote_copy(
        src_ref=mt_ref.at[:, pl.ds(frames - 128, 128)], dst_ref=mprev, send_sem=mp_sem.at[0], recv_sem=mp_sem.at[1],
        device_id=(v, right), device_id_type=MESH)
    mp.start()

    @pl.loop(0, blocks)
    def _(c):
        for copy in halo_copies(c):
            copy.start()

    @pl.when(p == 0)
    def _():
        in_rm[...] = jnp.zeros_like(in_rm)
        in_rs[...] = jnp.zeros_like(in_rs)

    @pl.when(p == n_tm - 1)
    def _():
        in_lm[...] = jnp.zeros_like(in_lm)
        in_ls[...] = jnp.zeros_like(in_ls)

    w = tissue_ref[...]
    w_high, w_low = split2(w)
    pad = jnp.zeros((5, cols), jnp.float32)
    wbuf[...] = jnp.concatenate([w_high, pad, w_low, pad], axis=0).astype(jnp.bfloat16)
    lane_at = lax.broadcasted_iota(jnp.int32, (8, frames), 1)
    later = jnp.where(p > 0, 1.0, 0.0).astype(jnp.float32)

    def derivative(base, before):
        return base - jnp.where(lane_at == 0, before * later, pltpu.roll(base, 1, 1))

    mp.wait()
    base = mt_ref[...]
    deriv = derivative(base, mprev[:, 127:128])
    conf_m = jnp.concatenate([base[:6], deriv[:6], (base * base)[:6], (deriv * deriv)[:6]], axis=0)
    cmb[...] = jnp.concatenate(split2(conf_m), axis=0).astype(jnp.bfloat16)
    sacc[...] = jnp.zeros_like(sacc)

    def scan_copy(src, dst, send, recv, r, target):
        return pltpu.make_async_remote_copy(
            src_ref=src.at[r], dst_ref=dst.at[r], send_sem=send.at[r], recv_sem=recv.at[r],
            device_id=(v, target), device_id_type=MESH)

    def forward(step, lag, count, own, ins, outs, sends, recvs):
        for way, (first_at, end_at, target) in enumerate(((p, n_tm - 1, right), (n_tm - 1 - p, 0, left))):
            r = step - lag * first_at

            @pl.when((r >= 0) & (r < count))
            def _():
                copy = scan_copy(outs[way], ins[way], sends[way], recvs[way], r, target)

                @pl.when(first_at > 0)
                def _():
                    copy.wait_recv()

                @pl.when(p != end_at)
                def _():
                    outs[way][r] = own[r] + ins[way][r]
                    copy.start()

    m_args = (own_m, (in_rm, in_lm), (out_rm, out_lm), (rm_send, lm_send), (rm_recv, lm_recv))
    s_args = (own_s, (in_rs, in_ls), (out_rs, out_ls), (rs_send, ls_send), (rs_recv, ls_recv))

    def y_copy(c):
        return pltpu.make_async_copy(y.at[c], y_out.at[:, lanes(c)], y_sem.at[c])

    @pl.loop(0, groups)
    def _(g):
        @pl.loop(0, 2)
        def _(k):
            c = 2 * g + k
            for copy in local_copies(c):
                copy.wait()
            for copy in halo_copies(c):
                copy.wait_recv()
            despike_block(xs, sp, y, ym1, c, frames)
            y_copy(c).start()

        block = jnp.concatenate([y[2 * g], y[2 * g + 1]], axis=1)
        high = block.astype(jnp.bfloat16)
        low = (block - high.astype(jnp.float32)).astype(jnp.bfloat16)
        yh[:, at(g)] = high
        yl[:, at(g)] = low
        wg = wbuf[:, at(g)]
        sacc[...] += nt(wg, high) + nt(wg, low)
        cross = nn(cmb[...], high) + nn(cmb[...], low)
        own_m[g] = cross[:24] + cross[24:]
        forward(g, LAG_M, groups, *m_args)

    parts = sacc[0:8] + sacc[8:16]
    edge = jnp.sum(ym1[0:1] * tissue_ref[...], axis=1, keepdims=True)
    pieces = [parts[0:3, 128 * b:128 * b + 128] for b in range(frames // 128)] + [jnp.broadcast_to(edge, (3, 128))]
    unused = sig.shape[0] - 3 * len(pieces)
    if unused:
        pieces.append(jnp.zeros((unused, 128), jnp.float32))
    sig[...] = jnp.concatenate(pieces, axis=0)

    def sig_copy(k):
        return pltpu.make_async_remote_copy(
            src_ref=sig, dst_ref=sig_in.at[k], send_sem=sig_send.at[k], recv_sem=sig_recv.at[k],
            device_id=(lax.rem(v + k + 1, n_vox), p), device_id_type=MESH)

    for k in range(n_vox - 1):
        sig_copy(k).start()

    steps_m = groups + LAG_M * (n_tm - 1)
    steps_s = groups + LAG_S * (n_tm - 1)
    early = min(groups + 2, steps_m)
    for step in range(groups, early):
        forward(step, LAG_M, groups, *m_args)

    total = sig[...]
    for k in range(n_vox - 1):
        sig_copy(k).wait()
        total = total + sig_in[k]
    total = total * (1.0 / float(cols * n_vox))
    nb = frames // 128
    base = jnp.concatenate([total[3 * b:3 * b + 3] for b in range(nb)], axis=1)
    base = jnp.concatenate([base, jnp.zeros((5, frames), jnp.float32)], axis=0)
    before = jnp.concatenate([total[3 * nb:3 * nb + 3, 0:1], jnp.zeros((5, 1), jnp.float32)], axis=0)
    deriv = derivative(base, before)
    conf_s = jnp.concatenate(
        [base[:3], deriv[:3], (base * base)[:3], (deriv * deriv)[:3], jnp.zeros((4, frames), jnp.float32)], axis=0)
    csb = jnp.concatenate(split2(conf_s), axis=0).astype(jnp.bfloat16)
    base = mt_ref[...]
    deriv = derivative(base, mprev[:, 127:128])
    conf_m = jnp.concatenate([base[:6], deriv[:6], (base * base)[:6], (deriv * deriv)[:6]], axis=0)
    conf = jnp.concatenate([conf_m, conf_s], axis=0)
    gram[...] = nt(conf, jnp.concatenate([conf, jnp.zeros((88, frames), jnp.float32)], axis=0), HIGHEST)

    def gram_copy(k):
        return pltpu.make_async_remote_copy(
            src_ref=gram, dst_ref=gram_in.at[k], send_sem=gr_send.at[k], recv_sem=gr_recv.at[k],
            device_id=(v, lax.rem(p + k + 1, n_tm)), device_id_type=MESH)

    for k in range(n_tm - 1):
        gram_copy(k).start()

    row_at = lax.broadcasted_iota(jnp.int32, (40, 128), 0)
    col_at = lax.broadcasted_iota(jnp.int32, (40, 128), 1)

    def eliminate(matrix, k):
        pivot_row = matrix[k:k + 1, :]
        pivot_col = matrix[:, k:k + 1]
        inverse = 1.0 / pivot_row[:, k:k + 1]
        scaled = jnp.where(col_at[0:1] == k, inverse, pivot_row * inverse)
        rest = jnp.where(col_at == k, 0.0, matrix)
        return jnp.where(row_at == k, scaled, rest - pivot_col * scaled)

    matrix = None
    done = 0
    gram_at = LAG_S
    for step in range(max(steps_s, steps_m - early)):
        if step < groups:
            part = pl.ds(step * WIDE, WIDE)
            cross = nn(csb, yh[:, part]) + nn(csb, yl[:, part])
            own_s[step] = cross[:16] + cross[16:]
        if step < steps_s:
            forward(step, LAG_S, groups, *s_args)
        if early + step < steps_m:
            forward(early + step, LAG_M, groups, *m_args)
        if step == gram_at:
            matrix = gram[...]
            for k in range(n_tm - 1):
                gram_copy(k).wait()
                matrix = matrix + gram_in[k]
        if step >= gram_at:
            for k in range(done, min(done + 3, 36)):
                matrix = eliminate(matrix, k)
            done = min(done + 3, 36)
        if step == gram_at - 1:
            conf48 = jnp.concatenate([conf, jnp.zeros((8, frames), jnp.float32)], axis=0)
            c_high, c_low = split2(conf48)
            cs_out[...] = jnp.transpose(jnp.concatenate([c_high, c_low, c_high], axis=0)).astype(jnp.bfloat16)
    for k in range(done, 36):
        matrix = eliminate(matrix, k)

    inv = matrix[:, :40]
    for g in range(groups):
        cross = jnp.concatenate(
            [own_m[g] + in_rm[g] + in_lm[g], own_s[g] + in_rs[g] + in_ls[g]], axis=0)
        coef = nn(inv, cross, HIGHEST)
        b_high, b_low = split2(jnp.concatenate([coef, jnp.zeros((8, WIDE), jnp.float32)], axis=0))
        bs_out[:, pl.ds(g * WIDE, WIDE)] = jnp.concatenate([b_high, b_high, b_low], axis=0).astype(jnp.bfloat16)

    @pl.loop(0, groups)
    def _(g):
        for k in range(2):
            y_copy(2 * g + k).wait()
            for copy in halo_copies(2 * g + k):
                copy.wait_send()
        for args in (m_args, s_args):
            for way, (end_at, target) in enumerate(((n_tm - 1, right), (0, left))):
                @pl.when(p != end_at)
                def _():
                    scan_copy(args[2][way], args[1][way], args[3][way], args[4][way], g, target).wait_send()


def apply_kernel(y_ref, cs_ref, bs_ref, out_ref):
    at = pl.ds(pl.multiple_of(pl.program_id(0) * APPLY, APPLY), APPLY)
    out_ref[...] = y_ref[:, at] - nn(cs_ref[...], bs_ref[:, at])


def local(n_vox, n_tm, series, spikes, motion, tissue):
    frames, cols = series.shape
    groups = cols // WIDE
    blocks = cols // 128
    packed = -(-3 * (frames // 128 + 1) // 8) * 8
    mt = jnp.pad(motion.T, ((0, 2), (0, 0)))
    f32, bf16 = jnp.float32, jnp.bfloat16
    vmem = pl.BlockSpec(memory_space=pltpu.VMEM)
    hbm = pl.BlockSpec(memory_space=pl.ANY)
    dma = pltpu.SemaphoreType.DMA
    sums_m = pltpu.VMEM((groups, 24, WIDE), f32)
    sums_s = pltpu.VMEM((groups, 16, WIDE), f32)
    y, cs, bs = pl.pallas_call(
        functools.partial(kernel, n_vox, n_tm),
        out_shape=(
            jax.ShapeDtypeStruct((frames, cols), f32),
            jax.ShapeDtypeStruct((frames, 144), bf16),
            jax.ShapeDtypeStruct((144, cols), bf16),
        ),
        in_specs=[hbm, hbm, vmem, vmem],
        out_specs=[hbm, vmem, vmem],
        scratch_shapes=[
            pltpu.VMEM((blocks, frames + 2 * HALO, 128), f32),
            pltpu.VMEM((blocks, frames + 2 * HALO, 128), jnp.int32),
            pltpu.VMEM((blocks, frames, 128), f32),
            pltpu.VMEM((8, cols), f32),
            pltpu.VMEM((frames, cols), bf16),
            pltpu.VMEM((frames, cols), bf16),
            pltpu.VMEM((8, 128), f32),
            sums_m, sums_m, sums_m, sums_m, sums_m,
            sums_s, sums_s, sums_s, sums_s, sums_s,
            pltpu.VMEM((packed, 128), f32),
            pltpu.VMEM((n_vox - 1, packed, 128), f32),
            pltpu.VMEM((40, 128), f32),
            pltpu.VMEM((n_tm - 1, 40, 128), f32),
            pltpu.VMEM((16, cols), bf16),
            pltpu.VMEM((48, frames), bf16),
            pltpu.VMEM((16, frames), f32),
            dma((2, blocks)), dma((4, blocks)), dma((4, blocks)), dma((2,)),
            dma((groups,)), dma((groups,)), dma((groups,)), dma((groups,)),
            dma((groups,)), dma((groups,)), dma((groups,)), dma((groups,)),
            dma((n_vox - 1,)), dma((n_vox - 1,)), dma((n_tm - 1,)), dma((n_tm - 1,)),
            dma((blocks,)),
        ],
        compiler_params=pltpu.CompilerParams(
            collective_id=0, has_side_effects=True, vmem_limit_bytes=48 * 1024 * 1024),
        cost_estimate=pl.CostEstimate(flops=10**9, bytes_accessed=12 * frames * cols, transcendentals=0),
        name="despike_and_fit",
    )(series, spikes, mt, tissue)
    return pl.pallas_call(
        apply_kernel,
        grid=(cols // APPLY,),
        out_shape=jax.ShapeDtypeStruct((frames, cols), f32),
        in_specs=[vmem, vmem, vmem],
        out_specs=pl.BlockSpec((frames, APPLY), lambda g: (0, g)),
        compiler_params=pltpu.CompilerParams(vmem_limit_bytes=32 * 1024 * 1024),
        name="apply_coefficients",
    )(y, cs, bs)


def solution(mesh):
    return jax.shard_map(
        functools.partial(local, mesh.shape["vox"], mesh.shape["tm"]),
        mesh=mesh,
        in_specs=(P("tm", "vox"), P("tm", "vox"), P("tm", None), P(None, "vox")),
        out_specs=P("tm", "vox"),
        check_vma=False,
    )
```
